32 devices in a mesh: gx: 16 (over z, x, core), gy: 2 (over y).
Axes of the slice: x: 2, y: 2, z: 4, core: 2. Of those that a mesh axis runs over, the one named last changes fastest.
Arguments:
- potential: float32 [3, 1, 4096, 256], P(None, None, 'gx', 'gy'), may hold values from -8 to 8
- labels: int32 [1, 4096, 256], P(None, 'gx', 'gy'), may hold values from 0 to 7
- principal: float32 [2, 8], replicated, may hold values from 0.5 to 16
- off_diagonal: float32 [3, 8], replicated, may hold values from -0.4 to 0.4
Outputs:
- updated: float32 [3, 1, 4096, 256], P(None, None, 'gx', 'gy')
The draws below stay inside these ranges and needn't reach their ends.
All inputs are finite; a program needn't handle non-finite values.
Results may differ from the reference program's by a relative error of at most 0.0017.
Values sent between devices are 32-bit elements; how exact they have to be, the bound alone decides.
A program may use at most 64 MiB of HBM per device.

```python
import math
import jax
import jax.numpy as jnp
from jax import lax

NX = 4096
CY = 128
NZ = 1
LOADS = 3
PHASES = 8
NY = 256


def draw_potential(key, part):
    key_rough, key_shift, key_angle = jax.random.split(key, 3)
    dims_all = (LOADS, NZ, NX, NY)
    rough_part = jax.random.truncated_normal(key_rough, -3.0, 3.0, dims_all, jnp.float32)
    shifted = jax.random.uniform(key_shift, (LOADS, NZ, 1, 1), jnp.float32, -1.5, 1.5)
    phase_angle = jax.random.uniform(key_angle, (LOADS, NZ, 1, 1), jnp.float32, -math.pi, math.pi)
    position = jnp.arange(NX, dtype=jnp.float32)[None, None, :, None]
    long_wave = 3.0 * jnp.sin(position * (2.0 * math.pi / NX) + phase_angle)
    return rough_part + shifted + long_wave


def draw_principal(key, part):
    key_along, key_across = jax.random.split(key)
    along_x = jnp.exp(jax.random.uniform(key_along, (1, PHASES), jnp.float32, math.log(8.0), math.log(16.0)))
    along_y = jnp.exp(jax.random.uniform(key_across, (1, PHASES), jnp.float32, math.log(0.5), math.log(16.0)))
    return jnp.concatenate([along_x, along_y], 0)


def plant(array, stream_key, least, high):
    shape = array.shape
    place = [jax.random.randint(jax.random.fold_in(stream_key, axis), (), 0, shape[axis]) for axis in range(len(shape))]
    array = array.at[tuple(place)].set(least)
    longest = shape.index(max(shape))
    place[longest] = (place[longest] + 1) % shape[longest]
    return array.at[tuple(place)].set(high)


def setup_inputs(seed: int = 0) -> dict:
    seeds = jax.random.split(jax.random.key(seed), 5)
    potential = draw_potential(jax.random.fold_in(seeds[4], 71), 0)
    labels = plant(jax.random.randint(seeds[1], (NZ, NX, NY), 0, PHASES), jax.random.fold_in(seeds[1], 1), 0, PHASES - 1).astype(jnp.int32)
    principal = draw_principal(jax.random.fold_in(seeds[4], 71), 0)
    off_diagonal = jnp.clip(jax.random.uniform(seeds[3], (3, PHASES), jnp.float32, -0.4, 0.4), -0.4, 0.4)
    return dict(potential=potential, labels=labels, principal=principal, off_diagonal=off_diagonal)


def harmonic(first, second):
    return 2.0 * first * second / (first + second)


def cyclic_reduce(sub_diag, main_diag, super_diag, forcing, axis_dim):
    extent = sub_diag.shape[axis_dim]
    stride = 1
    while stride < extent:
        low_before = jnp.roll(sub_diag, stride, axis_dim)
        main_before = jnp.roll(main_diag, stride, axis_dim)
        high_before = jnp.roll(super_diag, stride, axis_dim)
        rest_before = jnp.roll(forcing, stride, axis_dim + 1)
        low_after = jnp.roll(sub_diag, -stride, axis_dim)
        main_after = jnp.roll(main_diag, -stride, axis_dim)
        high_after = jnp.roll(super_diag, -stride, axis_dim)
        rest_after = jnp.roll(forcing, -stride, axis_dim + 1)
        factor_low = -sub_diag / main_before
        factor_high = -super_diag / main_after
        forcing = forcing + factor_low[None] * rest_before + factor_high[None] * rest_after
        main_diag = main_diag + factor_low * high_before + factor_high * low_after
        sub_diag = factor_low * low_before
        super_diag = factor_high * high_after
        stride = stride * 2
    return forcing / (sub_diag + main_diag + super_diag)[None]


def central(values, axis_dim):
    return 0.5 * (jnp.roll(values, -1, axis_dim) - jnp.roll(values, 1, axis_dim))


def reference(potential, labels, principal, off_diagonal):
    damping = 2.0 / (CY * CY)
    components = jnp.concatenate([principal, off_diagonal], 0)

    def one_plane(pair):
        plane_field, plane_labels = pair
        tensor = components[:, plane_labels]
        face_east = harmonic(tensor[0], jnp.roll(tensor[0], -1, 0))
        face_west = jnp.roll(face_east, 1, 0)
        source_x = jnp.stack([face_east - face_west, central(tensor[2], 0), central(tensor[3], 0)])
        half_step = cyclic_reduce(-face_west, damping + face_west + face_east, -face_east,
                                  damping * plane_field + source_x, 0)
        face_north = harmonic(tensor[1], jnp.roll(tensor[1], -1, 1))
        face_south = jnp.roll(face_north, 1, 1)
        source_y = jnp.stack([central(tensor[2], 1), face_north - face_south, central(tensor[4], 1)])
        return cyclic_reduce(-face_south, damping + face_south + face_north, -face_north,
                             damping * half_step + source_y, 1)

    result = lax.map(one_plane, (jnp.moveaxis(potential, 1, 0), labels))
    return jnp.moveaxis(result, 0, 1)
```

```python
import functools

import jax
import jax.numpy as jnp
from jax import lax
from jax.experimental import pallas as pl
from jax.experimental.pallas import tpu as pltpu
from jax.sharding import PartitionSpec as P

MESH = pl.DeviceIdType.MESH
ROWS = 16


def sublane(shape):
    return lax.broadcasted_iota(jnp.int32, shape, len(shape) - 2)


def turn(x, by):
    size = x.shape[0]
    by = by % size
    return x if by == 0 else pltpu.roll(x, by, 0)


def following(q, last):
    wrap = turn(q[0], -1)
    wrap = jnp.where(sublane(wrap.shape) == 7, last, wrap)
    return wrap[None] if q.shape[0] == 1 else jnp.concatenate([q[1:], wrap[None]], 0)


def preceding(q):
    wrap = turn(q[-1], 1)
    first = jnp.where(sublane(wrap.shape) == 0, 0.0, wrap)[None]
    return (first if q.shape[0] == 1 else jnp.concatenate([first, q[:-1]], 0)), wrap


def split(q):
    pairs = q.reshape((q.shape[0] // 2, 2) + q.shape[1:])
    return pairs[:, 0], pairs[:, 1]


def merge(even, odd):
    return jnp.stack([even, odd], 1).reshape((2 * even.shape[0],) + even.shape[1:])


def wide(parts):
    return parts[0] if len(parts) == 1 else jnp.concatenate(parts, -1)


def strided(ref, steps):
    return jnp.stack([ref[pl.ds(t, 8, stride=steps), :] for t in range(steps)], 0)


def strided_wide(ref, steps):
    return wide([strided(ref.at[c], steps) for c in range(ref.shape[0])])


def put_wide(ref, value):
    for c in range(ref.shape[0]):
        ref[c] = value[:, c * 128 : (c + 1) * 128]


def lookup(tab, row, labels):
    out = jnp.full(labels.shape, tab(row, 0), jnp.float32)
    for phase in range(1, 8):
        out = jnp.where(labels == phase, tab(row, phase), out)
    return out


def faces(k):
    nxt = following(k, k[0])
    e = 2.0 * k * nxt / (k + nxt)
    steps = k.shape[0]
    position = lax.broadcasted_iota(jnp.int32, k.shape, 0)
    return jnp.where((position == steps - 1) & (sublane(k.shape) == 7), 0.0, e)


def factor(e, damping):
    g = jnp.full(e.shape, damping, jnp.float32)
    levels = []
    g_end = jnp.zeros(e.shape[1:], jnp.float32)
    top = True
    while e.shape[0] > 1:
        e_even, e_odd = split(e)
        g_even, g_odd = split(g)
        r = 1.0 / (e_even + e_odd + g_odd)
        if top:
            is_end = (lax.broadcasted_iota(jnp.int32, r.shape, 0) == r.shape[0] - 1) & (sublane(r.shape) == 7)
            r = jnp.where(is_end, 0.0, r)
            right = jnp.where(is_end, 1.0, e_odd * r)
        else:
            right = e_odd * r
        left = e_even * r
        top = False
        levels.append((left, right, r))
        e = e_even * right
        moved, wrap = preceding(right * g_odd)
        g = g_even + left * g_odd + moved
        g_end = g_end + wrap
    e, g = e[0], g[0]
    sub = sublane(e.shape)
    for by in (1, 2, 4):
        chosen = sub % (2 * by) == by
        e_left = turn(e, by)
        r = jnp.where(chosen, 1.0 / (e_left + e + g), 0.0)
        left, right = e_left * r, e * r
        levels.append((left, right, r))
        e = e * turn(right, -by)
        wrap = turn(right * g, by)
        g = g + turn(left * g, -by) + jnp.where(sub == 0, 0.0, wrap)
        g_end = g_end + wrap
    return levels, e, g, g_end


def forward(levels, f):
    kept = []
    f_end = jnp.zeros(f.shape[1:], jnp.float32)
    for left, right, r in levels[:-3]:
        f_even, f_odd = split(f)
        kept.append(f_odd * r)
        moved, wrap = preceding(right * f_odd)
        f = f_even + left * f_odd + moved
        f_end = f_end + wrap
    f = f[0]
    sub = sublane(f.shape)
    for by, (left, right, r) in zip((1, 2, 4), levels[-3:]):
        kept.append(f * r)
        wrap = turn(right * f, by)
        f = f + turn(left * f, -by) + jnp.where(sub == 0, 0.0, wrap)
        f_end = f_end + wrap
    return kept, f, f_end


def backward(levels, kept, first, last):
    shape = kept[-1].shape
    sub = sublane(shape)
    v = jnp.broadcast_to(first, shape)
    last = jnp.broadcast_to(last, shape)
    for by, (left, right, r), own in zip((4, 2, 1), levels[:-4:-1], kept[:-4:-1]):
        after = jnp.where(sub >= 8 - by, last, turn(v, -by))
        v = jnp.where(sub % (2 * by) == by, own + left * turn(v, by) + right * after, v)
    v = v[None]
    for (left, right, r), own in zip(levels[:-3][::-1], kept[:-3][::-1]):
        odd = own + left * v + right * following(v, last)
        v = merge(v, odd)
    return v


def central(k):
    return 0.5 * (following(k, jnp.zeros_like(k[0])) - preceding(k)[0])


def put_record(box, me, e, g, g_end, fs, f_ends, edges):
    base = pl.multiple_of(me * ROWS, ROWS)
    rows = [e[0:1], g[0:1]] + [f[0:1] for f in fs] + [g_end[0:1]] + [f[0:1] for f in f_ends]
    rows += [k[0, 0:1] for k in edges] + [k[-1, 7:8] for k in edges]
    rows.append(jnp.zeros_like(rows[0]))
    rows = jnp.concatenate(rows, 0)
    for c in range(box.shape[0]):
        box[c, pl.ds(base, ROWS), :] = rows[:, c * 128 : (c + 1) * 128]


def copies(box, me, n, axis, send, recv):
    out = []
    for d in range(1, n):
        slot = box.at[:, pl.ds(pl.multiple_of(me * ROWS, ROWS), ROWS), :]
        out.append(
            pltpu.make_async_remote_copy(
                src_ref=slot,
                dst_ref=slot,
                send_sem=send.at[d],
                recv_sem=recv.at[d],
                device_id={axis: lax.rem(me + d, n)},
                device_id_type=MESH,
            )
        )
    return out


def interface(box, n, order, me, first_out, last_out):
    def get_part(q, c):
        if n >= 8:
            return box[c, pl.ds(q, n, stride=ROWS), :]
        sub = sublane((8, 128)) % n
        out = jnp.broadcast_to(box[c, q : q + 1, :], (8, 128))
        for i in range(1, n):
            out = jnp.where(sub == i, box[c, i * ROWS + q : i * ROWS + q + 1, :], out)
        return out

    def get(q):
        return wide([get_part(q, c) for c in range(box.shape[0])])

    e, g = get(0), get(1)
    f = [get(2 + i) for i in range(3)]
    g_end = get(5)
    f_end = [get(6 + i) for i in range(3)]
    head = [get(9 + i) for i in range(3)]
    tail = [get(12 + i) for i in range(3)]
    head_next = [turn(k, -1) for k in head]
    link = 2.0 * tail[0] * head_next[0] / (tail[0] + head_next[0])
    gain = [link, 0.5 * head_next[1], 0.5 * head_next[2]]
    loss = [turn(link, 1), turn(0.5 * tail[1], 1), turn(0.5 * tail[2], 1)]
    for i, which in enumerate(order):
        f[i] = f[i] - loss[which]
        f_end[i] = f_end[i] + gain[which]
    r = 1.0 / (e + link + g_end)
    left, right = e * r, link * r
    g = g + left * g_end + turn(right * g_end, 1)
    f = [a + left * b + turn(right * b, 1) for a, b in zip(f, f_end)]
    e = e * right
    by = 1
    while by < n:
        e_left = turn(e, by)
        s = 1.0 / (e_left + e + g)
        lo, hi = e_left * s, e * s
        g = g + turn(lo * g, -by) + turn(hi * g, by)
        f = [a + turn(lo * a, -by) + turn(hi * a, by) for a in f]
        e = e * turn(hi, -by)
        by *= 2
    inv = 1.0 / g
    size = g.shape[0]
    for i in range(3):
        v = f[i] * inv
        first_out[i * size : (i + 1) * size, :] = v
        last_out[i * size : (i + 1) * size, :] = r * f_end[i] + left * v + right * turn(v, -1)
    return [
        (first_out[pl.ds(i * size + me, 1), :], last_out[pl.ds(i * size + me, 1), :]) for i in range(3)
    ]


def kernel(nx, ny, damping, pot, lab, pri, off, out, box_x, box_y, labt, ft,
           first_x, last_x, first_y, last_y, send_x, recv_x, send_y, recv_y):
    me_x, me_y = lax.axis_index("gx"), lax.axis_index("gy")
    barrier = pltpu.get_barrier_semaphore()
    for d in range(1, nx):
        pl.semaphore_signal(barrier, inc=1, device_id={"gx": lax.rem(me_x + d, nx)}, device_id_type=MESH)
    for d in range(1, ny):
        pl.semaphore_signal(barrier, inc=1, device_id={"gy": lax.rem(me_y + d, ny)}, device_id_type=MESH)

    def tab(row, phase):
        return pri[row, phase] if row < 2 else off[row - 2, phase]

    rows, cols = lab.shape
    steps = rows // 8
    labels = strided(lab, steps)
    k, a, b = lookup(tab, 0, labels), lookup(tab, 2, labels), lookup(tab, 3, labels)
    e = faces(k)
    levels, e_in, g, g_end = factor(e, damping)
    source = [e - preceding(e)[0], central(a), central(b)]
    solved = [forward(levels, damping * strided(pot.at[i], steps) + source[i]) for i in range(3)]
    put_record(box_x, me_x, e_in, g, g_end, [s[1] for s in solved], [s[2] for s in solved], [k, a, b])
    pl.semaphore_wait(barrier, nx - 1 + ny - 1)
    sent_x = copies(box_x, me_x, nx, "gx", send_x, recv_x)
    for copy in sent_x:
        copy.start()

    lanes = labt.shape[0] * 128
    repeat = lanes // rows

    def across(q):
        flat = q.reshape(rows, cols)
        if repeat > 1:
            flat = jnp.concatenate([flat] * repeat, 0)
        return flat.T

    put_wide(labt, across(labels))
    ysteps = cols // 8
    labels_y = strided_wide(labt, ysteps)
    ky, ay, by = lookup(tab, 1, labels_y), lookup(tab, 2, labels_y), lookup(tab, 4, labels_y)
    ey = faces(ky)
    levels_y, ey_in, gy, gy_end = factor(ey, damping)
    source_y = [central(ay), ey - preceding(ey)[0], central(by)]

    for copy in sent_x:
        copy.wait_recv()
    ends = interface(box_x, nx, (0, 1, 2), me_x, first_x, last_x)
    solved_y = []
    for i in range(3):
        half = backward(levels, solved[i][0], *ends[i])
        put_wide(ft.at[i], across(half))
        solved_y.append(forward(levels_y, damping * strided_wide(ft.at[i], ysteps) + source_y[i]))
    put_record(box_y, me_y, ey_in, gy, gy_end, [s[1] for s in solved_y], [s[2] for s in solved_y], [ky, ay, by])
    sent_y = copies(box_y, me_y, ny, "gy", send_y, recv_y)
    for copy in sent_y:
        copy.start()
    for copy in sent_y:
        copy.wait_recv()
    ends = interface(box_y, ny, (1, 0, 2), me_y, first_y, last_y)
    for i in range(3):
        v = backward(levels_y, solved_y[i][0], *ends[i])
        for t in range(ysteps):
            for c in range(lanes // 128):
                ft[i, c, pl.ds(t, 8, stride=ysteps), :] = v[t, :, c * 128 : (c + 1) * 128]
        back = jnp.concatenate([ft[i, c].T for c in range(lanes // 128)], 0)[:rows].reshape(steps, 8, cols)
        for t in range(steps):
            out[i, pl.ds(t, 8, stride=steps), :] = back[t]
    for copy in sent_x + sent_y:
        copy.wait_send()


def local(potential, labels, principal, off_diagonal):
    nx, ny = lax.axis_size("gx"), lax.axis_size("gy")
    loads, _, rows, cols = potential.shape
    lanes = max(rows, 128)
    damping = 2.0 / (cols * cols)
    vmem = pl.BlockSpec(memory_space=pltpu.VMEM)
    smem = pl.BlockSpec(memory_space=pltpu.SMEM)
    result = pl.pallas_call(
        functools.partial(kernel, nx, ny, damping),
        out_shape=jax.ShapeDtypeStruct((loads, rows, cols), jnp.float32),
        in_specs=[vmem, vmem, smem, smem],
        out_specs=vmem,
        scratch_shapes=[
            pltpu.VMEM((1, nx * ROWS, cols), jnp.float32),
            pltpu.VMEM((lanes // 128, ny * ROWS, 128), jnp.float32),
            pltpu.VMEM((lanes // 128, cols, 128), jnp.int32),
            pltpu.VMEM((loads, lanes // 128, cols, 128), jnp.float32),
            pltpu.VMEM((loads * max(nx, 8), cols), jnp.float32),
            pltpu.VMEM((loads * max(nx, 8), cols), jnp.float32),
            pltpu.VMEM((loads * max(ny, 8), lanes), jnp.float32),
            pltpu.VMEM((loads * max(ny, 8), lanes), jnp.float32),
            pltpu.SemaphoreType.DMA((nx,)),
            pltpu.SemaphoreType.DMA((nx,)),
            pltpu.SemaphoreType.DMA((ny,)),
            pltpu.SemaphoreType.DMA((ny,)),
        ],
        compiler_params=pltpu.CompilerParams(
            collective_id=0, has_side_effects=True, vmem_limit_bytes=32 * 1024 * 1024
        ),
    )(potential.reshape(loads, rows, cols), labels.reshape(rows, cols), principal, off_diagonal)
    return result.reshape(potential.shape)


def solution(mesh):
    in_specs = (P(None, None, "gx", "gy"), P(None, "gx", "gy"), P(), P())
    out_specs = P(None, None, "gx", "gy")
    return jax.shard_map(local, mesh=mesh, in_specs=in_specs, out_specs=out_specs, check_vma=False)
```

```python
import functools

import jax
import jax.numpy as jnp
from jax import lax
from jax.experimental import pallas as pl
from jax.experimental.pallas import tpu as pltpu
from jax.sharding import PartitionSpec as P

MESH = pl.DeviceIdType.MESH
ROWS = 8


def sublane(shape):
    return lax.broadcasted_iota(jnp.int32, shape, len(shape) - 2)


def turn(x, by):
    size = x.shape[0]
    by = by % size
    return x if by == 0 else pltpu.roll(x, by, 0)


def following(q, last):
    wrap = turn(q[0], -1)
    wrap = jnp.where(sublane(wrap.shape) == 7, last, wrap)
    return wrap[None] if q.shape[0] == 1 else jnp.concatenate([q[1:], wrap[None]], 0)


def preceding(q):
    wrap = turn(q[-1], 1)
    first = jnp.where(sublane(wrap.shape) == 0, 0.0, wrap)[None]
    return (first if q.shape[0] == 1 else jnp.concatenate([first, q[:-1]], 0)), wrap


def split(q):
    pairs = q.reshape((q.shape[0] // 2, 2) + q.shape[1:])
    return pairs[:, 0], pairs[:, 1]


def merge(even, odd):
    return jnp.stack([even, odd], 1).reshape((2 * even.shape[0],) + even.shape[1:])


def wide(parts):
    return parts[0] if len(parts) == 1 else jnp.concatenate(parts, -1)


def strided(ref, steps):
    return jnp.stack([ref[pl.ds(t, 8, stride=steps), :] for t in range(steps)], 0)


def strided_wide(ref, steps):
    return wide([strided(ref.at[c], steps) for c in range(ref.shape[0])])


def put_wide(ref, value):
    for c in range(ref.shape[0]):
        ref[c] = value[:, c * 128 : (c + 1) * 128]


def lookup(tab, row, labels):
    out = jnp.broadcast_to(tab(row, 0), labels.shape)
    for phase in range(1, 8):
        out = jnp.where(labels == phase, jnp.broadcast_to(tab(row, phase), labels.shape), out)
    return out


def faces(k):
    nxt = following(k, k[0])
    e = 2.0 * k * nxt / (k + nxt)
    steps = k.shape[0]
    position = lax.broadcasted_iota(jnp.int32, k.shape, 0)
    return jnp.where((position == steps - 1) & (sublane(k.shape) == 7), 0.0, e)


def factor(e, damping):
    g = jnp.full(e.shape, damping, jnp.float32)
    levels = []
    g_end = jnp.zeros(e.shape[1:], jnp.float32)
    top = True
    while e.shape[0] > 1:
        e_even, e_odd = split(e)
        g_even, g_odd = split(g)
        r = 1.0 / (e_even + e_odd + g_odd)
        if top:
            is_end = (lax.broadcasted_iota(jnp.int32, r.shape, 0) == r.shape[0] - 1) & (sublane(r.shape) == 7)
            r = jnp.where(is_end, 0.0, r)
            right = jnp.where(is_end, 1.0, e_odd * r)
        else:
            right = e_odd * r
        left = e_even * r
        top = False
        levels.append((left, right, r))
        e = e_even * right
        moved, wrap = preceding(right * g_odd)
        g = g_even + left * g_odd + moved
        g_end = g_end + wrap
    e, g = e[0], g[0]
    sub = sublane(e.shape)
    for by in (1, 2, 4):
        chosen = sub % (2 * by) == by
        e_left = turn(e, by)
        r = jnp.where(chosen, 1.0 / (e_left + e + g), 0.0)
        left, right = e_left * r, e * r
        levels.append((left, right, r))
        e = e * turn(right, -by)
        wrap = turn(right * g, by)
        g = g + turn(left * g, -by) + jnp.where(sub == 0, 0.0, wrap)
        g_end = g_end + wrap
    return levels, e, g, g_end


def forward(levels, f):
    kept = []
    f_end = jnp.zeros(f.shape[1:], jnp.float32)
    for left, right, r in levels[:-3]:
        f_even, f_odd = split(f)
        kept.append(f_odd * r)
        moved, wrap = preceding(right * f_odd)
        f = f_even + left * f_odd + moved
        f_end = f_end + wrap
    f = f[0]
    sub = sublane(f.shape)
    for by, (left, right, r) in zip((1, 2, 4), levels[-3:]):
        kept.append(f * r)
        wrap = turn(right * f, by)
        f = f + turn(left * f, -by) + jnp.where(sub == 0, 0.0, wrap)
        f_end = f_end + wrap
    return kept, f, f_end


def backward(levels, kept, first, last):
    shape = kept[-1].shape
    sub = sublane(shape)
    v = jnp.broadcast_to(first, shape)
    last = jnp.broadcast_to(last, shape)
    for by, (left, right, r), own in zip((4, 2, 1), levels[:-4:-1], kept[:-4:-1]):
        after = jnp.where(sub >= 8 - by, last, turn(v, -by))
        v = jnp.where(sub % (2 * by) == by, own + left * turn(v, by) + right * after, v)
    v = v[None]
    for (left, right, r), own in zip(levels[:-3][::-1], kept[:-3][::-1]):
        odd = own + left * v + right * following(v, last)
        v = merge(v, odd)
    return v


def central(k):
    return 0.5 * (following(k, jnp.zeros_like(k[0])) - preceding(k)[0])


def put_record(box, me, rows):
    base = pl.multiple_of(me * len(rows), ROWS)
    rows = jnp.concatenate(rows, 0)
    for c in range(box.shape[0]):
        box[c, pl.ds(base, rows.shape[0]), :] = rows[:, c * 128 : (c + 1) * 128]


def matrix_rows(e, g, g_end, k, a):
    return [e[0:1], g[0:1], g_end[0:1], k[0, 0:1], k[-1, 7:8], a[0, 0:1], a[-1, 7:8], jnp.zeros_like(e[0:1])]


def forcing_rows(solved, b):
    return [s[1][0:1] for s in solved] + [s[2][0:1] for s in solved] + [b[0, 0:1], b[-1, 7:8]]


def copies(box, me, n, axis, send, recv):
    out = []
    rows = box.shape[1] // n
    for d in range(1, n):
        slot = box.at[:, pl.ds(pl.multiple_of(me * rows, ROWS), rows), :]
        out.append(
            pltpu.make_async_remote_copy(
                src_ref=slot,
                dst_ref=slot,
                send_sem=send.at[d],
                recv_sem=recv.at[d],
                device_id={axis: lax.rem(me + d, n)},
                device_id_type=MESH,
            )
        )
    return out


def get_row(box, n, q):
    parts = []
    rows = box.shape[1] // n
    for c in range(box.shape[0]):
        if n >= 8:
            parts.append(box[c, pl.ds(q, n, stride=rows), :])
            continue
        sub = sublane((8, 128)) % n
        out = jnp.broadcast_to(box[c, q : q + 1, :], (8, 128))
        for i in range(1, n):
            out = jnp.where(sub == i, box[c, i * rows + q : i * rows + q + 1, :], out)
        parts.append(out)
    return wide(parts)


def ring_factor(box, n):
    e, g, g_end, k_head, k_tail, a_head, a_tail = [get_row(box, n, q) for q in range(7)]
    k_next = turn(k_head, -1)
    link = 2.0 * k_tail * k_next / (k_tail + k_next)
    gain = [link, 0.5 * turn(a_head, -1)]
    loss = [turn(link, 1), turn(0.5 * a_tail, 1)]
    r = 1.0 / (e + link + g_end)
    left, right = e * r, link * r
    g = g + left * g_end + turn(right * g_end, 1)
    e = e * right
    levels = []
    by = 1
    while by < n:
        e_left = turn(e, by)
        s = 1.0 / (e_left + e + g)
        lo, hi = e_left * s, e * s
        levels.append((by, lo, hi))
        g = g + turn(lo * g, -by) + turn(hi * g, by)
        e = e * turn(hi, -by)
        by *= 2
    return gain, loss, r, left, right, levels, 1.0 / g


def ring_solve(box, n, skip, ring, order, me, first_out, last_out):
    gain, loss, r, left, right, levels, inv = ring
    f = [get_row(box, n, skip + q) for q in range(3)]
    f_end = [get_row(box, n, skip + q) for q in range(3, 6)]
    b_head, b_tail = get_row(box, n, skip + 6), get_row(box, n, skip + 7)
    gain = gain + [0.5 * turn(b_head, -1)]
    loss = loss + [turn(0.5 * b_tail, 1)]
    size = inv.shape[0]
    for i, which in enumerate(order):
        end = f_end[i] + gain[which]
        v = f[i] - loss[which] + left * end + turn(right * end, 1)
        for by, lo, hi in levels:
            v = v + turn(lo * v, -by) + turn(hi * v, by)
        v = v * inv
        first_out[i * size : (i + 1) * size, :] = v
        last_out[i * size : (i + 1) * size, :] = r * end + left * v + right * turn(v, -1)
    return [
        (first_out[pl.ds(i * size + me, 1), :], last_out[pl.ds(i * size + me, 1), :]) for i in range(3)
    ]


def kernel(nx, ny, damping, pot_hbm, lab_hbm, pri_hbm, off_hbm, out, pot, lab, pri, off, box_x, mat_y, box_y, labt, ft,
           first_x, last_x, first_y, last_y, send_x, recv_x, send_y, recv_y,
           send_my, recv_my, load):
    me_x, me_y = lax.axis_index("gx"), lax.axis_index("gy")
    barrier = pltpu.get_barrier_semaphore()
    for d in range(1, nx):
        pl.semaphore_signal(barrier, inc=1, device_id={"gx": lax.rem(me_x + d, nx)}, device_id_type=MESH)
    for d in range(1, ny):
        pl.semaphore_signal(barrier, inc=1, device_id={"gy": lax.rem(me_y + d, ny)}, device_id_type=MESH)

    loads = [
        pltpu.make_async_copy(src, dst, load.at[i])
        for i, (src, dst) in enumerate(((lab_hbm, lab), (pri_hbm, pri), (off_hbm, off), (pot_hbm, pot)))
    ]
    for copy in loads:
        copy.start()
    def tab(row, phase):
        ref, row = (pri, row) if row < 2 else (off, row - 2)
        return ref[row : row + 1, phase : phase + 1]

    rows, cols = lab.shape
    steps = rows // 8
    for copy in loads[:3]:
        copy.wait()
    labels = strided(lab, steps)
    k, a = lookup(tab, 0, labels), lookup(tab, 2, labels)
    e = faces(k)
    levels, e_in, g, g_end = factor(e, damping)
    b = lookup(tab, 3, labels)
    source = [e - preceding(e)[0], central(a), central(b)]
    loads[3].wait()
    solved = [forward(levels, damping * strided(pot.at[i], steps) + source[i]) for i in range(3)]
    put_record(box_x, me_x, matrix_rows(e_in, g, g_end, k, a) + forcing_rows(solved, b))
    pl.semaphore_wait(barrier, nx - 1 + ny - 1)
    sent_x = copies(box_x, me_x, nx, "gx", send_x, recv_x)
    for copy in sent_x:
        copy.start()

    lanes = labt.shape[0] * 128
    repeat = lanes // rows

    def across(q):
        flat = q.reshape(rows, cols)
        if repeat > 1:
            flat = jnp.concatenate([flat] * repeat, 0)
        return flat.T

    put_wide(labt, across(labels))
    ysteps = cols // 8
    labels_y = strided_wide(labt, ysteps)
    ky, ay, by = lookup(tab, 1, labels_y), lookup(tab, 2, labels_y), lookup(tab, 4, labels_y)
    ey = faces(ky)
    levels_y, ey_in, gy, gy_end = factor(ey, damping)
    put_record(mat_y, me_y, matrix_rows(ey_in, gy, gy_end, ky, ay))
    sent_my = copies(mat_y, me_y, ny, "gy", send_my, recv_my)
    for copy in sent_my:
        copy.start()
    source_y = [central(ay), ey - preceding(ey)[0], central(by)]

    for copy in sent_x:
        copy.wait_recv()
    ring_x = ring_factor(box_x, nx)
    ends = ring_solve(box_x, nx, ROWS, ring_x, (0, 1, 2), me_x, first_x, last_x)
    solved_y = []
    for i in range(3):
        half = backward(levels, solved[i][0], *ends[i])
        put_wide(ft.at[i], across(half))
        solved_y.append(forward(levels_y, damping * strided_wide(ft.at[i], ysteps) + source_y[i]))
    put_record(box_y, me_y, forcing_rows(solved_y, by))
    sent_y = copies(box_y, me_y, ny, "gy", send_y, recv_y)
    for copy in sent_y:
        copy.start()
    for copy in sent_my:
        copy.wait_recv()
    ring_y = ring_factor(mat_y, ny)
    for copy in sent_y:
        copy.wait_recv()
    ends = ring_solve(box_y, ny, 0, ring_y, (1, 0, 2), me_y, first_y, last_y)
    for i in range(3):
        v = backward(levels_y, solved_y[i][0], *ends[i])
        for t in range(ysteps):
            for c in range(lanes // 128):
                ft[i, c, pl.ds(t, 8, stride=ysteps), :] = v[t, :, c * 128 : (c + 1) * 128]
        back = jnp.concatenate([ft[i, c].T for c in range(lanes // 128)], 0)[:rows].reshape(steps, 8, cols)
        for t in range(steps):
            out[i, pl.ds(t, 8, stride=steps), :] = back[t]
    for copy in sent_x + sent_my + sent_y:
        copy.wait_send()


def local(potential, labels, principal, off_diagonal):
    nx, ny = lax.axis_size("gx"), lax.axis_size("gy")
    loads, _, rows, cols = potential.shape
    lanes = max(rows, 128)
    damping = 2.0 / (cols * cols)
    vmem = pl.BlockSpec(memory_space=pltpu.VMEM)
    hbm = pl.BlockSpec(memory_space=pltpu.HBM)
    result = pl.pallas_call(
        functools.partial(kernel, nx, ny, damping),
        out_shape=jax.ShapeDtypeStruct((loads, rows, cols), jnp.float32),
        in_specs=[hbm] * 4,
        out_specs=vmem,
        scratch_shapes=[
            pltpu.VMEM((loads, rows, cols), jnp.float32),
            pltpu.VMEM((rows, cols), jnp.int32),
            pltpu.VMEM(principal.shape, jnp.float32),
            pltpu.VMEM(off_diagonal.shape, jnp.float32),
            pltpu.VMEM((1, nx * 2 * ROWS, cols), jnp.float32),
            pltpu.VMEM((lanes // 128, ny * ROWS, 128), jnp.float32),
            pltpu.VMEM((lanes // 128, ny * ROWS, 128), jnp.float32),
            pltpu.VMEM((lanes // 128, cols, 128), jnp.int32),
            pltpu.VMEM((loads, lanes // 128, cols, 128), jnp.float32),
            pltpu.VMEM((loads * max(nx, 8), cols), jnp.float32),
            pltpu.VMEM((loads * max(nx, 8), cols), jnp.float32),
            pltpu.VMEM((loads * max(ny, 8), lanes), jnp.float32),
            pltpu.VMEM((loads * max(ny, 8), lanes), jnp.float32),
            pltpu.SemaphoreType.DMA((nx,)),
            pltpu.SemaphoreType.DMA((nx,)),
            pltpu.SemaphoreType.DMA((ny,)),
            pltpu.SemaphoreType.DMA((ny,)),
            pltpu.SemaphoreType.DMA((ny,)),
            pltpu.SemaphoreType.DMA((ny,)),
            pltpu.SemaphoreType.DMA((4,)),
        ],
        compiler_params=pltpu.CompilerParams(
            collective_id=0, has_side_effects=True, vmem_limit_bytes=32 * 1024 * 1024
        ),
    )(potential.reshape(loads, rows, cols), labels.reshape(rows, cols), principal, off_diagonal)
    return result.reshape(potential.shape)


def solution(mesh):
    in_specs = (P(None, None, "gx", "gy"), P(None, "gx", "gy"), P(), P())
    out_specs = P(None, None, "gx", "gy")
    return jax.shard_map(local, mesh=mesh, in_specs=in_specs, out_specs=out_specs, check_vma=False)
```
